128 devices in a mesh: ctx: 16 (over z_lo, y, core), section: 8 (over z_hi, x).
Axes of the slice: x: 4, y: 4, z: 4 (z_hi: 2, z_lo: 2; z = z_hi * 2 + z_lo), core: 2. Of those that a mesh axis runs over, the one named last changes fastest.
Arguments:
- queries: bfloat16 [8, 2048, 4096], P('section', 'ctx'), may hold values from -39 to 39, as said below
- key_vectors: bfloat16 [8, 2048, 512], P('section', 'ctx'), may hold values from -6 to 6
- value_vectors: bfloat16 [8, 2048, 512], P('section', 'ctx'), may hold values from -6 to 6
- cotangent: bfloat16 [8, 2048, 4096], P('section', 'ctx'), may hold values from -6 to 6
- slot_order: int32 [32], replicated, may hold values from 0 to 31, each once
Outputs:
- handed: bfloat16 [8, 2048, 4096], P('section', 'ctx')
- grad_query: bfloat16 [8, 2048, 4096], P('section', 'ctx')
- grad_key: float32 [8, 2048, 512], P('section', 'ctx')
- grad_value: float32 [8, 2048, 512], P('section', 'ctx')
The draws below stay inside these ranges and needn't reach their ends.
Inputs may be any that keep to these rules, and one draw needn't show every extreme that they name: `queries`: query entries lie in the stated range. slot_order is a permutation of the 32 blocks of the sequence.
All inputs are finite; a program needn't handle non-finite values.
Results may differ from the reference program's by a relative error of at most 0.017.
Values may be sent and summed in bfloat16 or wider, within the bound.
No kernel may reach another device: no remote copies, remote signals or barrier semaphores. Data moves between devices by JAX's collectives and lax.ppermute only.
A program may use at most 128 MiB of HBM per device.

```python
import math
import jax
import jax.numpy as jnp
from jax import lax

TOK_DEV = 128
BLK = 64
HEADS = 32
KV_HEADS = 4
HEAD_DIM = 128
TOKENS = 2048
SECTIONS = 8
N_CTX = 16


def draw_key_vectors(key, part):
    key = jax.random.fold_in(key, 3)
    shape_all = (SECTIONS, TOKENS, KV_HEADS, HEAD_DIM)
    result = jnp.clip(jax.random.normal(key, shape_all, jnp.float32), -6.0, 6.0)
    return result.reshape(SECTIONS, TOKENS, KV_HEADS * HEAD_DIM).astype(jnp.bfloat16)


def draw_queries(key, part):
    key = jax.random.fold_in(key, 5)
    shape_all = (SECTIONS, TOKENS, HEADS, HEAD_DIM)
    result = jnp.clip(jax.random.normal(key, shape_all, jnp.float32), -6.0, 6.0)
    return result.reshape(SECTIONS, TOKENS, HEADS * HEAD_DIM).astype(jnp.bfloat16)


def levels(stream_key, extent, pieces, least, high):
    def one(dim, parts):
        heights = jax.random.uniform(jax.random.fold_in(jax.random.fold_in(stream_key, 6), dim), (parts,), jnp.float32, least / len(pieces), high / len(pieces))
        return jnp.repeat(jnp.exp(heights), extent[dim] // parts).reshape((-1,) + (1,) * (len(extent) - dim - 1))

    gain = one(*pieces[0])
    for cut in pieces[1:]:
        gain = gain * one(*cut)
    return gain


def centred(rng, dims, width, bound, pieces=(), held_as=jnp.bfloat16):
    values = jax.random.normal(rng, dims, jnp.float32) * width
    if len(pieces) > 0:
        values = levels(rng, dims, pieces, -0.22, 0.18) * values
    return jnp.clip(values, min=-bound, max=bound).astype(held_as)


def setup_inputs(seed: int = 0) -> dict:
    key_of = jax.random.split(jax.random.key(seed), 6)
    queries = draw_queries(jax.random.fold_in(key_of[5], 71), 0)
    key_vectors = draw_key_vectors(jax.random.fold_in(key_of[5], 71), 0)
    value_vectors = centred(key_of[2], (SECTIONS, TOKENS, KV_HEADS * HEAD_DIM), 1.0, 6.0, ((0, 8), (1, 16)))
    cotangent = centred(key_of[3], (SECTIONS, TOKENS, HEADS * HEAD_DIM), 1.0, 6.0, ((0, 8), (1, 16)))
    slot_order = jax.random.permutation(key_of[4], TOKENS // BLK).astype(jnp.int32)
    return dict(queries=queries, key_vectors=key_vectors, value_vectors=value_vectors, cotangent=cotangent, slot_order=slot_order)


masked_score = -1e+30

def rounded(tensor):
    return lax.optimization_barrier(tensor.astype(jnp.bfloat16)).astype(jnp.float32)

def token_positions(slot_order):
    indices = jnp.arange(TOKENS, dtype=jnp.int32)
    return slot_order[indices // BLK] * BLK + indices % BLK

def one_section(operands, slot_order):
    query_all, key_all, value_all, grad_out = operands
    group_size = HEADS // KV_HEADS
    score_scale = 1.0 / math.sqrt(HEAD_DIM)
    key_heads = key_all.astype(jnp.float32).reshape(TOKENS, KV_HEADS, HEAD_DIM)
    value_heads = value_all.astype(jnp.float32).reshape(TOKENS, KV_HEADS, HEAD_DIM)
    positions = token_positions(slot_order)

    def block(totals, block_index):
        key_total, value_total = totals
        first_row = (block_index * TOK_DEV).astype(jnp.int32)
        query_block = lax.dynamic_slice_in_dim(query_all, first_row, TOK_DEV, 0).astype(jnp.float32)
        query_block = query_block.reshape(TOK_DEV, KV_HEADS, group_size, HEAD_DIM)
        grad_block = lax.dynamic_slice_in_dim(grad_out, first_row, TOK_DEV, 0).astype(jnp.float32)
        grad_block = grad_block.reshape(TOK_DEV, KV_HEADS, group_size, HEAD_DIM)
        query_pos = lax.dynamic_slice_in_dim(positions, first_row, TOK_DEV, 0)
        visible = (positions[None, :] <= query_pos[:, None])[:, None, None, :]
        scores = jnp.einsum('rgjd,ngd->rgjn', query_block, key_heads) * score_scale
        scores = jnp.where(visible, scores, masked_score)
        highest = lax.optimization_barrier(jnp.max(scores, axis=-1, keepdims=True))
        log_total = highest + jnp.log(lax.optimization_barrier(jnp.sum(jnp.exp(scores - highest), axis=-1, keepdims=True)))
        probabilities = jnp.exp(scores - log_total)
        weights = rounded(probabilities)
        attended = jnp.einsum('rgjn,ngd->rgjd', weights, value_heads).astype(jnp.bfloat16)
        row_delta = lax.optimization_barrier(jnp.sum(grad_block * attended.astype(jnp.float32), axis=-1, keepdims=True))
        grad_probs = jnp.einsum('rgjd,ngd->rgjn', grad_block, value_heads)
        grad_scores = rounded(probabilities * (grad_probs - row_delta))
        grad_query = (jnp.einsum('rgjn,ngd->rgjd', grad_scores, key_heads) * score_scale).astype(jnp.bfloat16)
        key_part = jnp.einsum('rgjn,rgjd->ngd', grad_scores, query_block) * score_scale
        value_part = jnp.einsum('rgjn,rgjd->ngd', weights, grad_block)
        totals = (key_total + rounded(key_part), value_total + rounded(value_part))
        return (totals, (attended.reshape(TOK_DEV, HEADS * HEAD_DIM), grad_query.reshape(TOK_DEV, HEADS * HEAD_DIM)))
    empty = jnp.zeros((TOKENS, KV_HEADS, HEAD_DIM), jnp.float32)
    totals, outputs = lax.scan(block, (empty, empty), jnp.arange(N_CTX, dtype=jnp.int32))
    attended = outputs[0].reshape(TOKENS, HEADS * HEAD_DIM)
    grad_query = outputs[1].reshape(TOKENS, HEADS * HEAD_DIM)
    grad_key = totals[0].reshape(TOKENS, KV_HEADS * HEAD_DIM)
    grad_value = totals[1].reshape(TOKENS, KV_HEADS * HEAD_DIM)
    return (attended, grad_query, grad_key, grad_value)

def reference(queries, key_vectors, value_vectors, cotangent, slot_order):
    incoming = jnp.roll(cotangent, -1, axis=0)
    outcome = lax.map(lambda operands: one_section(operands, slot_order), (queries, key_vectors, value_vectors, incoming))
    attended, grad_query, grad_key, grad_value = outcome
    return (jnp.roll(attended, 1, axis=0), grad_query, grad_key, grad_value)
```

```python
import functools
import math

import jax
import jax.numpy as jnp
from jax import lax
from jax.experimental import pallas as pl
from jax.experimental.pallas import tpu as pltpu
from jax.sharding import PartitionSpec as P

BLK = 64
HEADS = 32
KV_HEADS = 4
HEAD_DIM = 128
GROUP = HEADS // KV_HEADS
WIDE = GROUP * HEAD_DIM
ROWS = GROUP * BLK
CHUNK = 512
MASKED = -1e30
SCALE = 1.0 / math.sqrt(HEAD_DIM)
EXP2_SCALE = SCALE * math.log2(math.e)
VMEM_LIMIT = 56 * 2**20

f32 = jnp.float32
bf16 = jnp.bfloat16


def dot_nt(a, b):
    return lax.dot_general(a, b, (((1,), (1,)), ((), ())), preferred_element_type=f32)


def dot_nn(a, b):
    return lax.dot_general(a, b, (((1,), (0,)), ((), ())), preferred_element_type=f32)


def attention_kernel(
    which, slots, q_all, q_far, g_near, g_far, kv,
    o_near, o_far, dq_near, dq_far, dkv,
    q_near, ks, vs, kt, vt, st, eb, qs, gs, gt, dk_acc, dv_acc, m_ref, ot, dqt, sem,
):
    me = lax.axis_index("ctx")
    core = lax.rem(me, 2)
    col = pl.multiple_of((2 * core + which) * WIDE, WIDE)
    fetch = pltpu.make_async_copy(q_all.at[0, :, pl.ds(col, WIDE)], q_near, sem)
    fetch.start()
    blocks = kv.shape[0] // BLK
    tokens = kv.shape[0]

    for b in range(blocks):
        to = pl.multiple_of(slots[b] * BLK, BLK)
        ks[pl.ds(to, BLK), :] = kv[b * BLK : (b + 1) * BLK, 0:HEAD_DIM]
        vs[pl.ds(to, BLK), 0:HEAD_DIM] = kv[b * BLK : (b + 1) * BLK, HEAD_DIM : 2 * HEAD_DIM]
    lane = lax.broadcasted_iota(jnp.int32, (tokens, HEAD_DIM), 1)
    vs[:, HEAD_DIM : 2 * HEAD_DIM] = jnp.where(lane < 2, 1.0, 0.0).astype(bf16)
    for c in range(tokens // 256):
        part = slice(c * 256, (c + 1) * 256)
        kt[:, part] = ks[part, :].T
        vt[0:HEAD_DIM, part] = vs[part, 0:HEAD_DIM].T
    sub = lax.broadcasted_iota(jnp.int32, (16, tokens), 0)
    vt[HEAD_DIM : HEAD_DIM + 16, :] = jnp.where(sub == 0, 1.0, 0.0).astype(bf16)
    dk_acc[...] = jnp.zeros_like(dk_acc)
    dv_acc[...] = jnp.zeros_like(dv_acc)
    fetch.wait()

    for t in range(4):
        q, g, o, dq = (
            (q_near, g_near, o_near, dq_near) if t < 2 else (q_far, g_far, o_far, dq_far)
        )
        owner = me if t < 2 else me + 1 - 2 * core
        r0 = (t % 2) * BLK
        for h in range(GROUP):
            qs[h * BLK : (h + 1) * BLK, :] = q[r0 : r0 + BLK, h * HEAD_DIM : (h + 1) * HEAD_DIM]
            gs[h * BLK : (h + 1) * BLK, :] = g[r0 : r0 + BLK, h * HEAD_DIM : (h + 1) * HEAD_DIM]
        pos = slots[2 * owner + t % 2]
        last = (pos * BLK) // CHUNK
        qv = qs[...]

        def score(c, highest, masked):
            off = pl.multiple_of(c * CHUNK, CHUNK)
            s = dot_nt(ks[pl.ds(off, CHUNK), :], qv)
            if masked:
                key_pos = off + lax.broadcasted_iota(jnp.int32, (CHUNK, ROWS), 0)
                query_pos = pos * BLK + lax.broadcasted_iota(jnp.int32, (CHUNK, ROWS), 1) % BLK
                s = jnp.where(key_pos <= query_pos, s, MASKED)
            st[pl.ds(off, CHUNK), :] = s
            return jnp.maximum(highest, jnp.max(s.reshape(CHUNK // 8, 8, ROWS), axis=0))

        highest = lax.fori_loop(
            0, last, lambda c, m: score(c, m, False), jnp.full((8, ROWS), MASKED, f32)
        )
        highest = score(last, highest, True)
        m_ref[...] = jnp.max(highest, axis=0, keepdims=True)
        ot[...] = jnp.zeros_like(ot)

        def attend(c, _):
            off = pl.multiple_of(c * CHUNK, CHUNK)
            e = jnp.exp2((st[pl.ds(off, CHUNK), :] - m_ref[...]) * EXP2_SCALE).astype(bf16)
            eb[pl.ds(off, CHUNK), :] = e
            ot[...] += dot_nn(vt[:, pl.ds(off, CHUNK)], e)
            return 0

        lax.fori_loop(0, last + 1, attend, 0)
        inverse = 1.0 / ot[HEAD_DIM : HEAD_DIM + 1, :]
        attended_t = ot[0:HEAD_DIM, :] * inverse
        attended = attended_t.T.astype(bf16)
        for h in range(GROUP):
            o[r0 : r0 + BLK, h * HEAD_DIM : (h + 1) * HEAD_DIM] = attended[h * BLK : (h + 1) * BLK, :]
        scaled = (gs[...].T.astype(f32) * inverse).astype(bf16)
        gt[0:HEAD_DIM, :] = scaled
        gs[...] = scaled.T
        minus_delta = -jnp.sum(scaled.astype(f32) * attended_t, axis=0, keepdims=True)
        high = minus_delta.astype(bf16).astype(f32)
        low = minus_delta - high
        row = lax.broadcasted_iota(jnp.int32, (HEAD_DIM, ROWS), 0)
        gt[HEAD_DIM : 2 * HEAD_DIM, :] = jnp.where(
            row == 0, high, jnp.where(row == 1, low, 0.0)
        ).astype(bf16)
        dqt[...] = jnp.zeros_like(dqt)

        def backward(c, _):
            off = pl.multiple_of(c * CHUNK, CHUNK)
            centred = dot_nn(vs[pl.ds(off, CHUNK), :], gt[...])
            e = eb[pl.ds(off, CHUNK), :]
            ds = (e.astype(f32) * centred).astype(bf16)
            dv_acc[pl.ds(off, CHUNK), :] += dot_nn(e, gs[...])
            dk_acc[pl.ds(off, CHUNK), :] += dot_nn(ds, qs[...])
            dqt[...] += dot_nn(kt[:, pl.ds(off, CHUNK)], ds)
            return 0

        lax.fori_loop(0, last + 1, backward, 0)
        grad = (dqt[...] * SCALE).T.astype(bf16)
        for h in range(GROUP):
            dq[r0 : r0 + BLK, h * HEAD_DIM : (h + 1) * HEAD_DIM] = grad[h * BLK : (h + 1) * BLK, :]

    for b in range(blocks):
        at = pl.multiple_of(slots[b] * BLK, BLK)
        rows = slice(b * BLK, (b + 1) * BLK)
        dkv[rows, 0:HEAD_DIM] = (dk_acc[pl.ds(at, BLK), :] * SCALE).astype(bf16)
        dkv[rows, HEAD_DIM : 2 * HEAD_DIM] = dv_acc[pl.ds(at, BLK), :].astype(bf16)


def attention(which, slots, q_all, q_far, g_near, g_far, kv):
    local = q_far.shape[0]
    tokens = kv.shape[0]
    vmem = pl.BlockSpec(memory_space=pltpu.VMEM)
    piece = jax.ShapeDtypeStruct((local, WIDE), bf16)
    return pl.pallas_call(
        functools.partial(attention_kernel, which),
        out_shape=(piece,) * 4 + (jax.ShapeDtypeStruct((tokens, 2 * HEAD_DIM), bf16),),
        in_specs=[
            pl.BlockSpec(memory_space=pltpu.SMEM),
            pl.BlockSpec(memory_space=pl.ANY),
        ] + [vmem] * 4,
        out_specs=(vmem,) * 5,
        scratch_shapes=[
            pltpu.VMEM((local, WIDE), bf16),
            pltpu.VMEM((tokens, HEAD_DIM), bf16),
            pltpu.VMEM((tokens, 2 * HEAD_DIM), bf16),
            pltpu.VMEM((HEAD_DIM, tokens), bf16),
            pltpu.VMEM((HEAD_DIM + 16, tokens), bf16),
            pltpu.VMEM((tokens, ROWS), f32),
            pltpu.VMEM((tokens, ROWS), bf16),
            pltpu.VMEM((ROWS, HEAD_DIM), bf16),
            pltpu.VMEM((ROWS, HEAD_DIM), bf16),
            pltpu.VMEM((2 * HEAD_DIM, ROWS), bf16),
            pltpu.VMEM((tokens, HEAD_DIM), f32),
            pltpu.VMEM((tokens, HEAD_DIM), f32),
            pltpu.VMEM((1, ROWS), f32),
            pltpu.VMEM((HEAD_DIM + 16, ROWS), f32),
            pltpu.VMEM((HEAD_DIM, ROWS), f32),
            pltpu.SemaphoreType.DMA,
        ],
        compiler_params=pltpu.CompilerParams(vmem_limit_bytes=VMEM_LIMIT),
    )(slots, q_all, q_far, g_near, g_far, kv)


def join_kernel(near_a, far_a, near_b, far_b, out):
    core = lax.rem(lax.axis_index("ctx"), 2)
    for which, near, far in ((0, near_a, far_a), (1, near_b, far_b)):
        out[0, :, pl.ds(pl.multiple_of((2 * core + which) * WIDE, WIDE), WIDE)] = near[...]
        out[0, :, pl.ds(pl.multiple_of((2 - 2 * core + which) * WIDE, WIDE), WIDE)] = far[...]


def join(*pieces):
    vmem = pl.BlockSpec(memory_space=pltpu.VMEM)
    return pl.pallas_call(
        join_kernel,
        out_shape=jax.ShapeDtypeStruct((1, pieces[0].shape[0], HEADS * HEAD_DIM), bf16),
        in_specs=[vmem] * 4,
        out_specs=vmem,
        compiler_params=pltpu.CompilerParams(vmem_limit_bytes=VMEM_LIMIT),
    )(*pieces)


def total_kernel(local, part_a, part_b, dk, dv):
    sources = part_a.shape[0] // local
    for core in range(2):
        for which, part in ((0, part_a), (1, part_b)):
            total = jnp.zeros((local, 2 * HEAD_DIM), f32)
            for s in range(core, sources, 2):
                total = total + part[s * local : (s + 1) * local, :].astype(f32)
            head = 2 * core + which
            columns = slice(head * HEAD_DIM, (head + 1) * HEAD_DIM)
            dk[0, :, columns] = total[:, 0:HEAD_DIM]
            dv[0, :, columns] = total[:, HEAD_DIM : 2 * HEAD_DIM]


def totals(local, part_a, part_b):
    vmem = pl.BlockSpec(memory_space=pltpu.VMEM)
    return pl.pallas_call(
        functools.partial(total_kernel, local),
        out_shape=(jax.ShapeDtypeStruct((1, local, KV_HEADS * HEAD_DIM), f32),) * 2,
        in_specs=[vmem] * 2,
        out_specs=(vmem,) * 2,
        compiler_params=pltpu.CompilerParams(vmem_limit_bytes=VMEM_LIMIT),
    )(part_a, part_b)


def pair_swap(x):
    n = lax.axis_size("ctx")
    return lax.ppermute(x, "ctx", [(i, i ^ 1) for i in range(n)])


def to_section(x, step, swap):
    n, sections = lax.axis_size("ctx"), lax.axis_size("section")
    route = [
        (i * sections + s, (i ^ swap) * sections + (s + step) % sections)
        for i in range(n)
        for s in range(sections)
    ]
    return lax.ppermute(x, ("ctx", "section"), route)


def exchange(x):
    return lax.all_to_all(x, "ctx", 0, 0, tiled=True)


def body(queries, key_vectors, value_vectors, cotangent, slot_order):
    members = lax.axis_size("ctx")
    core = lax.rem(lax.axis_index("ctx"), 2)
    local = queries.shape[1]
    near = [2 * core + which for which in range(2)]
    far = [2 - 2 * core + which for which in range(2)]

    def part(x, head):
        return lax.dynamic_slice_in_dim(x[0], head * WIDE, WIDE, 1)

    def packed(which):
        halves = []
        for head in (which, 2 + which):
            columns = slice(head * HEAD_DIM, (head + 1) * HEAD_DIM)
            halves += [key_vectors[0][:, columns], value_vectors[0][:, columns]]
        two = jnp.stack(
            [jnp.concatenate(halves[0:2], axis=1), jnp.concatenate(halves[2:4], axis=1)]
        )
        return jnp.broadcast_to(two[None], (members // 2,) + two.shape).reshape(
            members * local, 2 * HEAD_DIM
        )

    kv = [exchange(packed(which)) for which in range(2)]
    q_far = [pair_swap(part(queries, far[which])) for which in range(2)]
    g_near = [to_section(part(cotangent, near[which]), -1, 0) for which in range(2)]
    g_far = [to_section(part(cotangent, far[which]), -1, 1) for which in range(2)]
    o_near, o_far, dq_near, dq_far, partial = [], [], [], [], []
    for which in range(2):
        a, b, c, d, e = attention(
            which, slot_order, queries, q_far[which], g_near[which], g_far[which], kv[which]
        )
        o_near.append(to_section(a, 1, 0))
        o_far.append(to_section(b, 1, 1))
        dq_near.append(c)
        dq_far.append(pair_swap(d))
        partial.append(exchange(e))
    handed = join(o_near[0], o_far[0], o_near[1], o_far[1])
    grad_query = join(dq_near[0], dq_far[0], dq_near[1], dq_far[1])
    grad_key, grad_value = totals(local, *partial)
    return handed, grad_query, grad_key, grad_value


def solution(mesh):
    tokens = P("section", "ctx", None)
    return jax.shard_map(
        body,
        mesh=mesh,
        in_specs=(tokens,) * 4 + (P(),),
        out_specs=(tokens,) * 4,
        check_vma=False,
    )
```

```python
import functools
import math

import jax
import jax.numpy as jnp
from jax import lax
from jax.experimental import pallas as pl
from jax.experimental.pallas import tpu as pltpu
from jax.sharding import PartitionSpec as P

BLK = 64
HEADS = 32
KV_HEADS = 4
HEAD_DIM = 128
GROUP = HEADS // KV_HEADS
WIDE = GROUP * HEAD_DIM
ROWS = GROUP * BLK
CHUNK = 256
MASKED = -1e30
SCALE = 1.0 / math.sqrt(HEAD_DIM)
EXP2_SCALE = SCALE * math.log2(math.e)
VMEM_LIMIT = 56 * 2**20

f32 = jnp.float32
bf16 = jnp.bfloat16


def dot_nt(a, b):
    return lax.dot_general(a, b, (((1,), (1,)), ((), ())), preferred_element_type=f32)


def dot_nn(a, b):
    return lax.dot_general(a, b, (((1,), (0,)), ((), ())), preferred_element_type=f32)


PLACES = ((0, 0, 4), (1, 0, 4), (2, 0, 4), (3, 0, 4))


def relative(me, planes, steps, cores):
    z, y, core = me // 8, me // 2 % 4, me % 2
    return (z + planes) % 2 * 8 + (y + steps) % 4 * 2 + (core + cores) % 2


def attention_kernel(
    which, slots, q_all, q_far, g_near, g_far, kv0, kv1, kv2, kv3,
    o_near, o_far, dq_near, dq_far, dkv0, dkv1, dkv2, dkv3,
    qa, ga, oa, dqa, ks, vs, kt, vt, st, eb, qs, gs, gt, dk_acc, dv_acc, m_ref, sem,
):
    me = lax.axis_index("ctx")
    core = lax.rem(me, 2)
    local = q_far.shape[0]
    col = pl.multiple_of((2 * core + which) * WIDE, WIDE)
    fetches = [
        pltpu.make_async_copy(q_all.at[0, :, pl.ds(col, WIDE)], qa.at[0:local], sem.at[0]),
        pltpu.make_async_copy(
            q_far.at[:, which * WIDE : (which + 1) * WIDE], qa.at[local : 2 * local], sem.at[1]
        ),
    ]
    for fetch in fetches:
        fetch.start()
    tokens = ks.shape[0]

    for (step, begin, end), part in zip(PLACES, (kv0, kv1, kv2, kv3)):
        for shard in range(begin, end):
            owner = relative(me, shard // 2, step, shard % 2)
            for b in range(2):
                to = pl.multiple_of(slots[2 * owner + b] * BLK, BLK)
                first = (2 * (shard - begin) + b) * BLK
                rows = slice(first, first + BLK)
                ks[pl.ds(to, BLK), :] = part[rows, 0:HEAD_DIM]
                vs[pl.ds(to, BLK), 0:HEAD_DIM] = part[rows, HEAD_DIM : 2 * HEAD_DIM]
    lane = lax.broadcasted_iota(jnp.int32, (tokens, HEAD_DIM), 1)
    vs[:, HEAD_DIM : 2 * HEAD_DIM] = jnp.where(lane < 2, 1.0, 0.0).astype(bf16)
    for c in range(tokens // 256):
        part = slice(c * 256, (c + 1) * 256)
        kt[:, part] = ks[part, :].T
        vt[0:HEAD_DIM, part] = vs[part, 0:HEAD_DIM].T
    sub = lax.broadcasted_iota(jnp.int32, (16, tokens), 0)
    vt[HEAD_DIM : HEAD_DIM + 16, :] = jnp.where(sub == 0, 1.0, 0.0).astype(bf16)
    dk_acc[...] = jnp.zeros_like(dk_acc)
    dv_acc[...] = jnp.zeros_like(dv_acc)
    ga[0:local, :] = g_near[...]
    ga[local : 2 * local, :] = g_far[...]
    for fetch in fetches:
        fetch.wait()

    def block(t, _):
        r0 = pl.multiple_of(t * BLK, BLK)
        for h in range(GROUP):
            rows, columns = slice(h * BLK, (h + 1) * BLK), slice(h * HEAD_DIM, (h + 1) * HEAD_DIM)
            qs[rows, :] = qa[pl.ds(r0, BLK), columns]
            gs[rows, :] = ga[pl.ds(r0, BLK), columns]
        owner = relative(me, 0, 0, t // 2)
        pos = slots[2 * owner + lax.rem(t, 2)]

        def run(seen):
            inside = seen - CHUNK
            if inside:
                s = dot_nt(ks[0:inside, :], qs[...])
                st[0:inside, :] = s
                highest = jnp.max(s.reshape(inside // 8, 8, ROWS), axis=0)
            s = dot_nt(ks[inside:seen, :], qs[...])
            key_pos = inside + lax.broadcasted_iota(jnp.int32, (CHUNK, ROWS), 0)
            query_pos = pos * BLK + lax.broadcasted_iota(jnp.int32, (CHUNK, ROWS), 1) % BLK
            s = jnp.where(key_pos <= query_pos, s, MASKED)
            st[inside:seen, :] = s
            edge = jnp.max(s.reshape(CHUNK // 8, 8, ROWS), axis=0)
            if inside:
                edge = jnp.maximum(edge, highest)
            m_ref[...] = jnp.max(edge, axis=0, keepdims=True)

            e = jnp.exp2((st[0:seen, :] - m_ref[...]) * EXP2_SCALE).astype(bf16)
            eb[0:seen, :] = e
            weighted = dot_nn(vt[:, 0:seen], e)
            inverse = 1.0 / weighted[HEAD_DIM : HEAD_DIM + 1, :]
            attended_t = weighted[0:HEAD_DIM, :] * inverse
            attended = attended_t.astype(bf16).T
            for h in range(GROUP):
                oa[pl.ds(r0, BLK), h * HEAD_DIM : (h + 1) * HEAD_DIM] = (
                    attended[h * BLK : (h + 1) * BLK, :]
                )

            scaled = (gs[...].T.astype(f32) * inverse).astype(bf16)
            gt[0:HEAD_DIM, :] = scaled
            gs[...] = scaled.T
            minus_delta = -jnp.sum(scaled.astype(f32) * attended_t, axis=0, keepdims=True)
            high = minus_delta.astype(bf16).astype(f32)
            low = minus_delta - high
            row = lax.broadcasted_iota(jnp.int32, (HEAD_DIM, ROWS), 0)
            gt[HEAD_DIM : 2 * HEAD_DIM, :] = jnp.where(
                row == 0, high, jnp.where(row == 1, low, 0.0)
            ).astype(bf16)

            centred = dot_nn(vs[0:seen, :], gt[...])
            e = eb[0:seen, :]
            ds = (e.astype(f32) * centred).astype(bf16)
            dv_acc[0:seen, :] += dot_nn(e, gs[...])
            dk_acc[0:seen, :] += dot_nn(ds, qs[...])
            grad = (dot_nn(kt[:, 0:seen], ds) * SCALE).astype(bf16).T
            for h in range(GROUP):
                dqa[pl.ds(r0, BLK), h * HEAD_DIM : (h + 1) * HEAD_DIM] = (
                    grad[h * BLK : (h + 1) * BLK, :]
                )
            return 0

        branches = [functools.partial(run, (i + 1) * CHUNK) for i in range(tokens // CHUNK)]
        return lax.switch((pos * BLK) // CHUNK, branches)

    lax.fori_loop(0, 4, block, 0)
    o_near[...] = oa[0:local, :]
    o_far[...] = oa[local : 2 * local, :]
    dq_near[...] = dqa[0:local, :]
    dq_far[...] = dqa[local : 2 * local, :]
    for (step, begin, end), part in zip(PLACES, (dkv0, dkv1, dkv2, dkv3)):
        for shard in range(begin, end):
            owner = relative(me, shard // 2, step, shard % 2)
            for b in range(2):
                at = pl.multiple_of(slots[2 * owner + b] * BLK, BLK)
                first = (2 * (shard - begin) + b) * BLK
                rows = slice(first, first + BLK)
                part[rows, 0:HEAD_DIM] = (dk_acc[pl.ds(at, BLK), :] * SCALE).astype(bf16)
                part[rows, HEAD_DIM : 2 * HEAD_DIM] = dv_acc[pl.ds(at, BLK), :].astype(bf16)


def attention(which, slots, q_all, q_far, g_near, g_far, kv):
    local = q_far.shape[0]
    tokens = sum(part.shape[0] for part in kv)
    vmem = pl.BlockSpec(memory_space=pltpu.VMEM)
    piece = jax.ShapeDtypeStruct((local, WIDE), bf16)
    return pl.pallas_call(
        functools.partial(attention_kernel, which),
        out_shape=(piece,) * 4 + tuple(jax.ShapeDtypeStruct(part.shape, bf16) for part in kv),
        in_specs=[
            pl.BlockSpec(memory_space=pltpu.SMEM),
            pl.BlockSpec(memory_space=pl.ANY),
            pl.BlockSpec(memory_space=pl.ANY),
        ] + [vmem] * 6,
        out_specs=(vmem,) * 8,
        scratch_shapes=[
            pltpu.VMEM((2 * local, WIDE), bf16),
            pltpu.VMEM((2 * local, WIDE), bf16),
            pltpu.VMEM((2 * local, WIDE), bf16),
            pltpu.VMEM((2 * local, WIDE), bf16),
            pltpu.VMEM((tokens, HEAD_DIM), bf16),
            pltpu.VMEM((tokens, 2 * HEAD_DIM), bf16),
            pltpu.VMEM((HEAD_DIM, tokens), bf16),
            pltpu.VMEM((HEAD_DIM + 16, tokens), bf16),
            pltpu.VMEM((tokens, ROWS), f32),
            pltpu.VMEM((tokens, ROWS), bf16),
            pltpu.VMEM((ROWS, HEAD_DIM), bf16),
            pltpu.VMEM((ROWS, HEAD_DIM), bf16),
            pltpu.VMEM((2 * HEAD_DIM, ROWS), bf16),
            pltpu.VMEM((tokens, HEAD_DIM), f32),
            pltpu.VMEM((tokens, HEAD_DIM), f32),
            pltpu.VMEM((1, ROWS), f32),
            pltpu.SemaphoreType.DMA((2,)),
        ],
        cost_estimate=pl.CostEstimate(
            flops=2 * 10**10, bytes_accessed=8 * 2**20, transcendentals=2**23
        ),
        compiler_params=pltpu.CompilerParams(vmem_limit_bytes=VMEM_LIMIT),
    )(slots, q_all, q_far, g_near, g_far, *kv)


def from_ctx(x, planes, steps, cores):
    n = lax.axis_size("ctx")
    return lax.ppermute(x, "ctx", [(relative(i, planes, steps, cores), i) for i in range(n)])


def pair_swap(x):
    return from_ctx(x, 0, 0, 1)


def to_section(x, step, swap):
    n, sections = lax.axis_size("ctx"), lax.axis_size("section")
    route = [
        (i * sections + s, (i ^ swap) * sections + (s + step) % sections)
        for i in range(n)
        for s in range(sections)
    ]
    return lax.ppermute(x, ("ctx", "section"), route)


def after(x, first):
    return lax.optimization_barrier((x, first))[0]


def body(queries, key_vectors, value_vectors, cotangent, slot_order):
    core = lax.rem(lax.axis_index("ctx"), 2)
    near = [2 * core + which for which in range(2)]
    far = [2 - 2 * core + which for which in range(2)]

    def part(x, head):
        return lax.dynamic_slice_in_dim(x[0], head * WIDE, WIDE, 1)

    def heads_of(which_core):
        pieces = []
        for head in (2 * which_core, 2 * which_core + 1):
            columns = slice(head * HEAD_DIM, (head + 1) * HEAD_DIM)
            pieces += [key_vectors[0][:, columns], value_vectors[0][:, columns]]
        return jnp.concatenate(pieces, axis=1)

    first, second = heads_of(0), heads_of(1)
    mine = jnp.where(core == 0, first, second)
    theirs = jnp.where(core == 0, second, first)
    shards = [mine, from_ctx(theirs, 0, 0, 1), from_ctx(mine, 1, 0, 0), from_ctx(theirs, 1, 0, 1)]
    q_far = pair_swap(lax.dynamic_slice_in_dim(queries[0], far[0] * WIDE, 2 * WIDE, 1))
    kv, g_near, g_far = [], [], []
    for which in range(2):
        columns = slice(2 * which * HEAD_DIM, 2 * (which + 1) * HEAD_DIM)
        plane = jnp.concatenate([shard[:, columns] for shard in shards], axis=0)
        if which:
            plane = after(plane, kv[0])
        kv.append([plane] + [from_ctx(plane, 0, steps, 0) for steps in (1, 2, 3)])
        sends = [part(cotangent, near[which]), part(cotangent, far[which])]
        sends = after(sends, (g_near[0], g_far[0]) if which else shards[2])
        g_near.append(to_section(sends[0], -1, 0))
        g_far.append(to_section(sends[1], -1, 1))
    local = queries.shape[1]
    o_near, o_far, dq_near, dq_far, partial = [], [], [], [], []
    for which in range(2):
        a, b, c, d, *pieces = attention(
            which, slot_order, queries, q_far, g_near[which], g_far[which], kv[which]
        )
        if which:
            pieces, a, b, partial[0], o_near[0], o_far[0], dq_far[0] = lax.optimization_barrier(
                (pieces, a, b, partial[0], o_near[0], o_far[0], dq_far[0])
            )
        o_near.append(to_section(a, 1, 0))
        o_far.append(to_section(b, 1, 1))
        dq_near.append(c)
        dq_far.append(d)
        partial.append(
            [
                pieces[0],
                from_ctx(pieces[1], 0, -1, 0),
                from_ctx(pieces[2], 0, -2, 0),
                from_ctx(pieces[3], 0, -3, 0),
            ]
        )

    def quarter(i):
        sums = []
        for place in partial:
            total = jnp.zeros((local, 2 * HEAD_DIM), f32)
            for (_, begin, end), x in zip(PLACES, place):
                if begin <= i < end:
                    total = total + x[(i - begin) * local : (i - begin + 1) * local].astype(f32)
            sums.append(total)
        return sums

    packed = lax.optimization_barrier(
        [jnp.concatenate(quarter(i), axis=1).astype(bf16) for i in (1, 2, 3)]
    )

    def sent(i, planes, cores):
        got = from_ctx(packed[i - 1], planes, 0, cores).astype(f32)
        return got[:, : 2 * HEAD_DIM], got[:, 2 * HEAD_DIM :]

    own = [x + y for x, y in zip(quarter(0), sent(2, 1, 0))]
    other = [x + y for x, y in zip(sent(1, 0, 1), sent(3, 1, 1))]

    def joined(near, far):
        low = jnp.concatenate(near + far, axis=1)
        high = jnp.concatenate(far + near, axis=1)
        return jnp.where(core == 0, low, high)[None]

    handed = joined(o_near, o_far)
    grad_query = joined(dq_near, [pair_swap(x) for x in dq_far])
    grad_key, grad_value = (
        joined([x[:, columns] for x in own], [x[:, columns] for x in other])
        for columns in (slice(0, HEAD_DIM), slice(HEAD_DIM, 2 * HEAD_DIM))
    )
    return handed, grad_query, grad_key, grad_value


def solution(mesh):
    tokens = P("section", "ctx", None)
    return jax.shard_map(
        body,
        mesh=mesh,
        in_specs=(tokens,) * 4 + (P(),),
        out_specs=(tokens,) * 4,
        check_vma=False,
    )
```

```python
import functools
import math

import jax
import jax.numpy as jnp
from jax import lax
from jax.experimental import pallas as pl
from jax.experimental.pallas import tpu as pltpu
from jax.sharding import PartitionSpec as P

BLK = 64
HEADS = 32
KV_HEADS = 4
HEAD_DIM = 128
GROUP = HEADS // KV_HEADS
WIDE = GROUP * HEAD_DIM
ROWS = GROUP * BLK
CHUNK = 256
MASKED = -1e30
SCALE = 1.0 / math.sqrt(HEAD_DIM)
EXP2_SCALE = SCALE * math.log2(math.e)
VMEM_LIMIT = 56 * 2**20

f32 = jnp.float32
bf16 = jnp.bfloat16


def dot_nt(a, b):
    return lax.dot_general(a, b, (((1,), (1,)), ((), ())), preferred_element_type=f32)


def dot_nn(a, b):
    return lax.dot_general(a, b, (((1,), (0,)), ((), ())), preferred_element_type=f32)


PLACES = ((0, 0, 4), (1, 0, 4), (2, 0, 4), (3, 0, 4))


def relative(me, planes, steps, cores):
    z, y, core = me // 8, me // 2 % 4, me % 2
    return (z + planes) % 2 * 8 + (y + steps) % 4 * 2 + (core + cores) % 2


def attention_kernel(
    which, slots, q_all, q_far, g_near, g_far, kv0, kv1, kv2, kv3,
    o_near, o_far, dq_near, dq_far, dkv0, dkv1, dkv2, dkv3,
    qa, ga, oa, dqa, ks, vs, kt, vt, st, eb, qs, gs, gt, dk_acc, dv_acc, m_ref, sem,
):
    me = lax.axis_index("ctx")
    core = lax.rem(me, 2)
    local = q_far.shape[0]
    col = pl.multiple_of((2 * core + which) * WIDE, WIDE)
    fetches = [
        pltpu.make_async_copy(q_all.at[0, :, pl.ds(col, WIDE)], qa.at[0:local], sem.at[0]),
        pltpu.make_async_copy(
            q_far.at[:, which * WIDE : (which + 1) * WIDE], qa.at[local : 2 * local], sem.at[1]
        ),
    ]
    for fetch in fetches:
        fetch.start()
    tokens = ks.shape[0]

    for (step, begin, end), part in zip(PLACES, (kv0, kv1, kv2, kv3)):
        for shard in range(begin, end):
            owner = relative(me, shard // 2, step, shard % 2)
            for b in range(2):
                to = pl.multiple_of(slots[2 * owner + b] * BLK, BLK)
                first = (2 * (shard - begin) + b) * BLK
                rows = slice(first, first + BLK)
                ks[pl.ds(to, BLK), :] = part[rows, 0:HEAD_DIM]
                vs[pl.ds(to, BLK), 0:HEAD_DIM] = part[rows, HEAD_DIM : 2 * HEAD_DIM]
    lane = lax.broadcasted_iota(jnp.int32, (tokens, HEAD_DIM), 1)
    vs[:, HEAD_DIM : 2 * HEAD_DIM] = jnp.where(lane < 2, 1.0, 0.0).astype(bf16)
    for c in range(tokens // 256):
        part = slice(c * 256, (c + 1) * 256)
        kt[:, part] = ks[part, :].T
        vt[0:HEAD_DIM, part] = vs[part, 0:HEAD_DIM].T
    sub = lax.broadcasted_iota(jnp.int32, (16, tokens), 0)
    vt[HEAD_DIM : HEAD_DIM + 16, :] = jnp.where(sub == 0, 1.0, 0.0).astype(bf16)
    dk_acc[...] = jnp.zeros_like(dk_acc)
    dv_acc[...] = jnp.zeros_like(dv_acc)
    ga[0:local, :] = g_near[...]
    ga[local : 2 * local, :] = g_far[...]
    for fetch in fetches:
        fetch.wait()

    def block(t, _):
        r0 = pl.multiple_of(t * BLK, BLK)
        for h in range(GROUP):
            rows, columns = slice(h * BLK, (h + 1) * BLK), slice(h * HEAD_DIM, (h + 1) * HEAD_DIM)
            qs[rows, :] = qa[pl.ds(r0, BLK), columns]
            gs[rows, :] = ga[pl.ds(r0, BLK), columns]
        owner = relative(me, 0, 0, t // 2)
        pos = slots[2 * owner + lax.rem(t, 2)]

        def run(seen):
            inside = seen - CHUNK
            if inside:
                s = dot_nt(ks[0:inside, :], qs[...])
                st[0:inside, :] = s
                highest = jnp.max(s.reshape(inside // 8, 8, ROWS), axis=0)
            s = dot_nt(ks[inside:seen, :], qs[...])
            key_pos = inside + lax.broadcasted_iota(jnp.int32, (CHUNK, ROWS), 0)
            query_pos = pos * BLK + lax.broadcasted_iota(jnp.int32, (CHUNK, ROWS), 1) % BLK
            s = jnp.where(key_pos <= query_pos, s, MASKED)
            st[inside:seen, :] = s
            edge = jnp.max(s.reshape(CHUNK // 8, 8, ROWS), axis=0)
            if inside:
                edge = jnp.maximum(edge, highest)
            m_ref[...] = jnp.max(edge, axis=0, keepdims=True)

            e = jnp.exp2((st[0:seen, :] - m_ref[...]) * EXP2_SCALE).astype(bf16)
            eb[0:seen, :] = e
            weighted = dot_nn(vt[:, 0:seen], e)
            inverse = 1.0 / weighted[HEAD_DIM : HEAD_DIM + 1, :]
            attended_t = weighted[0:HEAD_DIM, :] * inverse
            attended = attended_t.astype(bf16).T
            for h in range(GROUP):
                oa[pl.ds(r0, BLK), h * HEAD_DIM : (h + 1) * HEAD_DIM] = (
                    attended[h * BLK : (h + 1) * BLK, :]
                )

            scaled = (gs[...].T.astype(f32) * inverse).astype(bf16)
            gt[0:HEAD_DIM, :] = scaled
            gs[...] = scaled.T
            minus_delta = -jnp.sum(scaled.astype(f32) * attended_t, axis=0, keepdims=True)
            high = minus_delta.astype(bf16).astype(f32)
            low = minus_delta - high
            row = lax.broadcasted_iota(jnp.int32, (HEAD_DIM, ROWS), 0)
            gt[HEAD_DIM : 2 * HEAD_DIM, :] = jnp.where(
                row == 0, high, jnp.where(row == 1, low, 0.0)
            ).astype(bf16)

            centred = dot_nn(vs[0:seen, :], gt[...])
            e = eb[0:seen, :]
            ds = (e.astype(f32) * centred).astype(bf16)
            dv_acc[0:seen, :] += dot_nn(e, gs[...])
            dk_acc[0:seen, :] += dot_nn(ds, qs[...])
            grad = (dot_nn(kt[:, 0:seen], ds) * SCALE).astype(bf16).T
            for h in range(GROUP):
                dqa[pl.ds(r0, BLK), h * HEAD_DIM : (h + 1) * HEAD_DIM] = (
                    grad[h * BLK : (h + 1) * BLK, :]
                )
            return 0

        branches = [functools.partial(run, (i + 1) * CHUNK) for i in range(tokens // CHUNK)]
        return lax.switch((pos * BLK) // CHUNK, branches)

    lax.fori_loop(0, 4, block, 0)
    o_near[...] = oa[0:local, :]
    o_far[...] = oa[local : 2 * local, :]
    dq_near[...] = dqa[0:local, :]
    dq_far[...] = dqa[local : 2 * local, :]
    for (step, begin, end), part in zip(PLACES, (dkv0, dkv1, dkv2, dkv3)):
        for shard in range(begin, end):
            owner = relative(me, shard // 2, step, shard % 2)
            for b in range(2):
                at = pl.multiple_of(slots[2 * owner + b] * BLK, BLK)
                first = (2 * (shard - begin) + b) * BLK
                rows = slice(first, first + BLK)
                part[rows, 0:HEAD_DIM] = (dk_acc[pl.ds(at, BLK), :] * SCALE).astype(bf16)
                part[rows, HEAD_DIM : 2 * HEAD_DIM] = dv_acc[pl.ds(at, BLK), :].astype(bf16)


def attention(which, slots, q_all, q_far, g_near, g_far, kv):
    local = q_far.shape[0]
    tokens = sum(part.shape[0] for part in kv)
    vmem = pl.BlockSpec(memory_space=pltpu.VMEM)
    piece = jax.ShapeDtypeStruct((local, WIDE), bf16)
    return pl.pallas_call(
        functools.partial(attention_kernel, which),
        out_shape=(piece,) * 4 + tuple(jax.ShapeDtypeStruct(part.shape, bf16) for part in kv),
        in_specs=[
            pl.BlockSpec(memory_space=pltpu.SMEM),
            pl.BlockSpec(memory_space=pl.ANY),
            pl.BlockSpec(memory_space=pl.ANY),
        ] + [vmem] * 6,
        out_specs=(vmem,) * 8,
        scratch_shapes=[
            pltpu.VMEM((2 * local, WIDE), bf16),
            pltpu.VMEM((2 * local, WIDE), bf16),
            pltpu.VMEM((2 * local, WIDE), bf16),
            pltpu.VMEM((2 * local, WIDE), bf16),
            pltpu.VMEM((tokens, HEAD_DIM), bf16),
            pltpu.VMEM((tokens, 2 * HEAD_DIM), bf16),
            pltpu.VMEM((HEAD_DIM, tokens), bf16),
            pltpu.VMEM((HEAD_DIM + 16, tokens), bf16),
            pltpu.VMEM((tokens, ROWS), f32),
            pltpu.VMEM((tokens, ROWS), bf16),
            pltpu.VMEM((ROWS, HEAD_DIM), bf16),
            pltpu.VMEM((ROWS, HEAD_DIM), bf16),
            pltpu.VMEM((2 * HEAD_DIM, ROWS), bf16),
            pltpu.VMEM((tokens, HEAD_DIM), f32),
            pltpu.VMEM((tokens, HEAD_DIM), f32),
            pltpu.VMEM((1, ROWS), f32),
            pltpu.SemaphoreType.DMA((2,)),
        ],
        cost_estimate=pl.CostEstimate(
            flops=2 * 10**10, bytes_accessed=8 * 2**20, transcendentals=2**23
        ),
        compiler_params=pltpu.CompilerParams(vmem_limit_bytes=VMEM_LIMIT),
    )(slots, q_all, q_far, g_near, g_far, *kv)


def from_ctx(x, planes, steps, cores):
    n = lax.axis_size("ctx")
    return lax.ppermute(x, "ctx", [(relative(i, planes, steps, cores), i) for i in range(n)])


def pair_swap(x):
    return from_ctx(x, 0, 0, 1)


def to_section(x, step, swap):
    n, sections = lax.axis_size("ctx"), lax.axis_size("section")
    route = [
        (i * sections + s, (i ^ swap) * sections + (s + step) % sections)
        for i in range(n)
        for s in range(sections)
    ]
    return lax.ppermute(x, ("ctx", "section"), route)


def after(x, first):
    return lax.optimization_barrier((x, first))[0]


def body(queries, key_vectors, value_vectors, cotangent, slot_order):
    core = lax.rem(lax.axis_index("ctx"), 2)
    near = [2 * core + which for which in range(2)]
    far = [2 - 2 * core + which for which in range(2)]

    def part(x, head):
        return lax.dynamic_slice_in_dim(x[0], head * WIDE, WIDE, 1)

    def heads_of(which_core):
        pieces = []
        for head in (2 * which_core, 2 * which_core + 1):
            columns = slice(head * HEAD_DIM, (head + 1) * HEAD_DIM)
            pieces += [key_vectors[0][:, columns], value_vectors[0][:, columns]]
        return jnp.concatenate(pieces, axis=1)

    first, second = heads_of(0), heads_of(1)
    mine = jnp.where(core == 0, first, second)
    theirs = jnp.where(core == 0, second, first)
    shards = [mine, from_ctx(theirs, 0, 0, 1), from_ctx(mine, 1, 0, 0), from_ctx(theirs, 1, 0, 1)]
    q_far = lax.dynamic_slice_in_dim(queries[0], far[0] * WIDE, 2 * WIDE, 1)
    kv, g_near, g_far = [], [], []
    for which in range(2):
        columns = slice(2 * which * HEAD_DIM, 2 * (which + 1) * HEAD_DIM)
        plane = jnp.concatenate([shard[:, columns] for shard in shards], axis=0)
        if which:
            plane = after(plane, kv[0][3])
        else:
            q_far = pair_swap(after(q_far, plane))
        kv.append([plane] + [from_ctx(plane, 0, steps, 0) for steps in (1, 2, 3)])
        sends = [part(cotangent, near[which]), part(cotangent, far[which])]
        sends = after(sends, g_near[0] if which else q_far)
        g_near.append(to_section(sends[0], -1, 0))
        g_far.append(to_section(sends[1], -1, 1))
    local = queries.shape[1]
    o_near, o_far, dq_near, dq_far, partial = [], [], [], [], []
    for which in range(2):
        a, b, c, d, *pieces = attention(
            which, slot_order, queries, q_far, g_near[which], g_far[which], kv[which]
        )
        if which:
            pieces, a, b, partial[0], o_near[0], o_far[0], dq_far[0] = lax.optimization_barrier(
                (pieces, a, b, partial[0], o_near[0], o_far[0], dq_far[0])
            )
        o_near.append(to_section(a, 1, 0))
        o_far.append(to_section(b, 1, 1))
        dq_near.append(c)
        dq_far.append(d)
        partial.append(
            [
                pieces[0],
                from_ctx(pieces[1], 0, -1, 0),
                from_ctx(pieces[2], 0, -2, 0),
                from_ctx(pieces[3], 0, -3, 0),
            ]
        )

    def quarter(i):
        sums = []
        for place in partial:
            total = jnp.zeros((local, 2 * HEAD_DIM), f32)
            for (_, begin, end), x in zip(PLACES, place):
                if begin <= i < end:
                    total = total + x[(i - begin) * local : (i - begin + 1) * local].astype(f32)
            sums.append(total)
        return sums

    packed = lax.optimization_barrier(
        [jnp.concatenate(quarter(i), axis=1).astype(bf16) for i in (1, 2, 3)]
    )

    def sent(i, planes, cores):
        got = from_ctx(packed[i - 1], planes, 0, cores).astype(f32)
        return got[:, : 2 * HEAD_DIM], got[:, 2 * HEAD_DIM :]

    own = [x + y for x, y in zip(quarter(0), sent(2, 1, 0))]
    other = [x + y for x, y in zip(sent(1, 0, 1), sent(3, 1, 1))]

    def joined(near, far):
        low = jnp.concatenate(near + far, axis=1)
        high = jnp.concatenate(far + near, axis=1)
        return jnp.where(core == 0, low, high)[None]

    o_near[1], o_far[1] = after((o_near[1], o_far[1]), (own, other))
    handed = joined(o_near, o_far)
    grad_query = joined(dq_near, [pair_swap(x) for x in dq_far])
    grad_key, grad_value = (
        joined([x[:, columns] for x in own], [x[:, columns] for x in other])
        for columns in (slice(0, HEAD_DIM), slice(HEAD_DIM, 2 * HEAD_DIM))
    )
    return handed, grad_query, grad_key, grad_value


def solution(mesh):
    tokens = P("section", "ctx", None)
    return jax.shard_map(
        body,
        mesh=mesh,
        in_specs=(tokens,) * 4 + (P(),),
        out_specs=(tokens,) * 4,
        check_vma=False,
    )
```

```python
import functools
import math

import jax
import jax.numpy as jnp
from jax import lax
from jax.experimental import pallas as pl
from jax.experimental.pallas import tpu as pltpu
from jax.sharding import PartitionSpec as P

BLK = 64
HEADS = 32
KV_HEADS = 4
HEAD_DIM = 128
GROUP = HEADS // KV_HEADS
WIDE = GROUP * HEAD_DIM
ROWS = GROUP * BLK
CHUNK = 256
MASKED = -1e30
SCALE = 1.0 / math.sqrt(HEAD_DIM)
EXP2_SCALE = SCALE * math.log2(math.e)
VMEM_LIMIT = 56 * 2**20

f32 = jnp.float32
bf16 = jnp.bfloat16


def dot_nt(a, b):
    return lax.dot_general(a, b, (((1,), (1,)), ((), ())), preferred_element_type=f32)


def dot_nn(a, b):
    return lax.dot_general(a, b, (((1,), (0,)), ((), ())), preferred_element_type=f32)


PLACES = ((0, 0, 4), (1, 0, 4), (2, 0, 4), (3, 0, 4))


def relative(me, planes, steps, cores):
    z, y, core = me // 8, me // 2 % 4, me % 2
    return (z + planes) % 2 * 8 + (y + steps) % 4 * 2 + (core + cores) % 2


def attention_kernel(
    which, slots, q_all, q_far, g_near, g_far, kv0, kv1, kv2, kv3,
    o_near, o_far, dq_near, dq_far, dkv0, dkv1, dkv2, dkv3,
    qa, ga, oa, dqa, ks, vs, kt, vt, st, eb, qs, gs, gt, dk_acc, dv_acc, m_ref, sem,
):
    me = lax.axis_index("ctx")
    core = lax.rem(me, 2)
    local = q_far.shape[0]
    col = pl.multiple_of((2 * core + which) * WIDE, WIDE)
    fetches = [
        pltpu.make_async_copy(q_all.at[0, :, pl.ds(col, WIDE)], qa.at[0:local], sem.at[0]),
        pltpu.make_async_copy(
            q_far.at[:, which * WIDE : (which + 1) * WIDE], qa.at[local : 2 * local], sem.at[1]
        ),
    ]
    for fetch in fetches:
        fetch.start()
    tokens = ks.shape[0]

    for (step, begin, end), part in zip(PLACES, (kv0, kv1, kv2, kv3)):
        for shard in range(begin, end):
            owner = relative(me, shard // 2, step, shard % 2)
            for b in range(2):
                to = pl.multiple_of(slots[2 * owner + b] * BLK, BLK)
                first = (2 * (shard - begin) + b) * BLK
                rows = slice(first, first + BLK)
                ks[pl.ds(to, BLK), :] = part[rows, 0:HEAD_DIM]
                vs[pl.ds(to, BLK), 0:HEAD_DIM] = part[rows, HEAD_DIM : 2 * HEAD_DIM]
    lane = lax.broadcasted_iota(jnp.int32, (tokens, HEAD_DIM), 1)
    vs[:, HEAD_DIM : 2 * HEAD_DIM] = jnp.where(lane < 2, 1.0, 0.0).astype(bf16)
    for c in range(tokens // 256):
        part = slice(c * 256, (c + 1) * 256)
        kt[:, part] = ks[part, :].T
        vt[0:HEAD_DIM, part] = vs[part, 0:HEAD_DIM].T
    sub = lax.broadcasted_iota(jnp.int32, (16, tokens), 0)
    vt[HEAD_DIM : HEAD_DIM + 16, :] = jnp.where(sub == 0, 1.0, 0.0).astype(bf16)
    dk_acc[...] = jnp.zeros_like(dk_acc)
    dv_acc[...] = jnp.zeros_like(dv_acc)
    ga[0:local, :] = g_near[...]
    ga[local : 2 * local, :] = g_far[...]
    for fetch in fetches:
        fetch.wait()

    def block(t, _):
        r0 = pl.multiple_of(t * BLK, BLK)
        for h in range(GROUP):
            rows, columns = slice(h * BLK, (h + 1) * BLK), slice(h * HEAD_DIM, (h + 1) * HEAD_DIM)
            qs[rows, :] = qa[pl.ds(r0, BLK), columns]
            gs[rows, :] = ga[pl.ds(r0, BLK), columns]
        owner = relative(me, 0, 0, t // 2)
        pos = slots[2 * owner + lax.rem(t, 2)]

        def run(seen):
            inside = seen - CHUNK
            if inside:
                s = dot_nt(ks[0:inside, :], qs[...])
                st[0:inside, :] = s
                highest = jnp.max(s.reshape(inside // 8, 8, ROWS), axis=0)
            s = dot_nt(ks[inside:seen, :], qs[...])
            key_pos = inside + lax.broadcasted_iota(jnp.int32, (CHUNK, ROWS), 0)
            query_pos = pos * BLK + lax.broadcasted_iota(jnp.int32, (CHUNK, ROWS), 1) % BLK
            s = jnp.where(key_pos <= query_pos, s, MASKED)
            st[inside:seen, :] = s
            edge = jnp.max(s.reshape(CHUNK // 8, 8, ROWS), axis=0)
            if inside:
                edge = jnp.maximum(edge, highest)
            m_ref[...] = jnp.max(edge, axis=0, keepdims=True)

            e = jnp.exp2((st[0:seen, :] - m_ref[...]) * EXP2_SCALE).astype(bf16)
            eb[0:seen, :] = e
            weighted = dot_nn(vt[:, 0:seen], e)
            inverse = 1.0 / weighted[HEAD_DIM : HEAD_DIM + 1, :]
            attended_t = weighted[0:HEAD_DIM, :] * inverse
            attended = attended_t.astype(bf16).T
            for h in range(GROUP):
                oa[pl.ds(r0, BLK), h * HEAD_DIM : (h + 1) * HEAD_DIM] = (
                    attended[h * BLK : (h + 1) * BLK, :]
                )

            scaled = (gs[...].T.astype(f32) * inverse).astype(bf16)
            gt[0:HEAD_DIM, :] = scaled
            gs[...] = scaled.T
            minus_delta = -jnp.sum(scaled.astype(f32) * attended_t, axis=0, keepdims=True)
            high = minus_delta.astype(bf16).astype(f32)
            low = minus_delta - high
            row = lax.broadcasted_iota(jnp.int32, (HEAD_DIM, ROWS), 0)
            gt[HEAD_DIM : 2 * HEAD_DIM, :] = jnp.where(
                row == 0, high, jnp.where(row == 1, low, 0.0)
            ).astype(bf16)

            centred = dot_nn(vs[0:seen, :], gt[...])
            e = eb[0:seen, :]
            ds = (e.astype(f32) * centred).astype(bf16)
            dv_acc[0:seen, :] += dot_nn(e, gs[...])
            dk_acc[0:seen, :] += dot_nn(ds, qs[...])
            grad = (dot_nn(kt[:, 0:seen], ds) * SCALE).astype(bf16).T
            for h in range(GROUP):
                dqa[pl.ds(r0, BLK), h * HEAD_DIM : (h + 1) * HEAD_DIM] = (
                    grad[h * BLK : (h + 1) * BLK, :]
                )
            return 0

        branches = [functools.partial(run, (i + 1) * CHUNK) for i in range(tokens // CHUNK)]
        return lax.switch((pos * BLK) // CHUNK, branches)

    lax.fori_loop(0, 4, block, 0)
    o_near[...] = oa[0:local, :]
    o_far[...] = oa[local : 2 * local, :]
    dq_near[...] = dqa[0:local, :]
    dq_far[...] = dqa[local : 2 * local, :]
    for (step, begin, end), part in zip(PLACES, (dkv0, dkv1, dkv2, dkv3)):
        for shard in range(begin, end):
            owner = relative(me, shard // 2, step, shard % 2)
            for b in range(2):
                at = pl.multiple_of(slots[2 * owner + b] * BLK, BLK)
                first = (2 * (shard - begin) + b) * BLK
                rows = slice(first, first + BLK)
                part[rows, 0:HEAD_DIM] = (dk_acc[pl.ds(at, BLK), :] * SCALE).astype(bf16)
                part[rows, HEAD_DIM : 2 * HEAD_DIM] = dv_acc[pl.ds(at, BLK), :].astype(bf16)


def attention(which, slots, q_all, q_far, g_near, g_far, kv):
    local = q_far.shape[0]
    tokens = sum(part.shape[0] for part in kv)
    vmem = pl.BlockSpec(memory_space=pltpu.VMEM)
    piece = jax.ShapeDtypeStruct((local, WIDE), bf16)
    return pl.pallas_call(
        functools.partial(attention_kernel, which),
        out_shape=(piece,) * 4 + tuple(jax.ShapeDtypeStruct(part.shape, bf16) for part in kv),
        in_specs=[
            pl.BlockSpec(memory_space=pltpu.SMEM),
            pl.BlockSpec(memory_space=pl.ANY),
            pl.BlockSpec(memory_space=pl.ANY),
        ] + [vmem] * 6,
        out_specs=(vmem,) * 8,
        scratch_shapes=[
            pltpu.VMEM((2 * local, WIDE), bf16),
            pltpu.VMEM((2 * local, WIDE), bf16),
            pltpu.VMEM((2 * local, WIDE), bf16),
            pltpu.VMEM((2 * local, WIDE), bf16),
            pltpu.VMEM((tokens, HEAD_DIM), bf16),
            pltpu.VMEM((tokens, 2 * HEAD_DIM), bf16),
            pltpu.VMEM((HEAD_DIM, tokens), bf16),
            pltpu.VMEM((HEAD_DIM + 16, tokens), bf16),
            pltpu.VMEM((tokens, ROWS), f32),
            pltpu.VMEM((tokens, ROWS), bf16),
            pltpu.VMEM((ROWS, HEAD_DIM), bf16),
            pltpu.VMEM((ROWS, HEAD_DIM), bf16),
            pltpu.VMEM((2 * HEAD_DIM, ROWS), bf16),
            pltpu.VMEM((tokens, HEAD_DIM), f32),
            pltpu.VMEM((tokens, HEAD_DIM), f32),
            pltpu.VMEM((1, ROWS), f32),
            pltpu.SemaphoreType.DMA((2,)),
        ],
        cost_estimate=pl.CostEstimate(
            flops=2 * 10**10, bytes_accessed=8 * 2**20, transcendentals=2**23
        ),
        compiler_params=pltpu.CompilerParams(vmem_limit_bytes=VMEM_LIMIT),
    )(slots, q_all, q_far, g_near, g_far, *kv)


def from_ctx(x, planes, steps, cores):
    n = lax.axis_size("ctx")
    return lax.ppermute(x, "ctx", [(relative(i, planes, steps, cores), i) for i in range(n)])


def pair_swap(x):
    return from_ctx(x, 0, 0, 1)


def to_section(x, step, swap):
    n, sections = lax.axis_size("ctx"), lax.axis_size("section")
    route = [
        (i * sections + s, (i ^ swap) * sections + (s + step) % sections)
        for i in range(n)
        for s in range(sections)
    ]
    return lax.ppermute(x, ("ctx", "section"), route)


def after(x, first):
    return lax.optimization_barrier((x, first))[0]


def body(queries, key_vectors, value_vectors, cotangent, slot_order):
    core = lax.rem(lax.axis_index("ctx"), 2)
    near = [2 * core + which for which in range(2)]
    far = [2 - 2 * core + which for which in range(2)]

    def part(x, head):
        return lax.dynamic_slice_in_dim(x[0], head * WIDE, WIDE, 1)

    def heads_of(which_core):
        pieces = []
        for head in (2 * which_core, 2 * which_core + 1):
            columns = slice(head * HEAD_DIM, (head + 1) * HEAD_DIM)
            pieces += [key_vectors[0][:, columns], value_vectors[0][:, columns]]
        return jnp.concatenate(pieces, axis=1)

    first, second = heads_of(0), heads_of(1)
    mine = jnp.where(core == 0, first, second)
    theirs = jnp.where(core == 0, second, first)
    shards = [mine, from_ctx(theirs, 0, 0, 1), from_ctx(mine, 1, 0, 0), from_ctx(theirs, 1, 0, 1)]
    q_far = lax.dynamic_slice_in_dim(queries[0], far[0] * WIDE, 2 * WIDE, 1)
    kv, g_near, g_far = [], [], []
    for which in range(2):
        columns = slice(2 * which * HEAD_DIM, 2 * (which + 1) * HEAD_DIM)
        plane = jnp.concatenate([shard[:, columns] for shard in shards], axis=0)
        if which:
            plane = after(plane, kv[0][3])
        else:
            q_far = pair_swap(after(q_far, plane))
        kv.append([plane] + [from_ctx(plane, 0, steps, 0) for steps in (1, 2, 3)])
        sends = [part(cotangent, near[which]), part(cotangent, far[which])]
        sends = after(sends, g_near[0] if which else q_far)
        g_near.append(to_section(sends[0], -1, 0))
        g_far.append(to_section(sends[1], -1, 1))
    local = queries.shape[1]
    o_near, o_far, dq_near, dq_far, partial = [], [], [], [], []
    for which in range(2):
        a, b, c, d, *pieces = attention(
            which, slot_order, queries, q_far, g_near[which], g_far[which], kv[which]
        )
        if which:
            pieces, a, b, partial[0], o_near[0], o_far[0], dq_far[0] = lax.optimization_barrier(
                (pieces, a, b, partial[0], o_near[0], o_far[0], dq_far[0])
            )
        o_near.append(to_section(a, 1, 0))
        o_far.append(to_section(b, 1, 1))
        dq_near.append(c)
        dq_far.append(d)
        partial.append(
            [
                pieces[0],
                from_ctx(pieces[1], 0, -1, 0),
                from_ctx(pieces[2], 0, -2, 0),
                from_ctx(pieces[3], 0, -3, 0),
            ]
        )

    def quarter(i):
        sums = []
        for place in partial:
            total = jnp.zeros((local, 2 * HEAD_DIM), f32)
            for (_, begin, end), x in zip(PLACES, place):
                if begin <= i < end:
                    total = total + x[(i - begin) * local : (i - begin + 1) * local].astype(f32)
            sums.append(total)
        return sums

    packed = lax.optimization_barrier(
        [jnp.concatenate(quarter(i), axis=1).astype(bf16) for i in (1, 2, 3)]
    )

    def sent(i, planes, cores):
        return from_ctx(packed[i - 1], planes, 0, cores)

    def halves(x):
        return x[:, : 2 * HEAD_DIM].astype(f32), x[:, 2 * HEAD_DIM :].astype(f32)

    def joined(near, far):
        low = jnp.concatenate(near + far, axis=1)
        high = jnp.concatenate(far + near, axis=1)
        return jnp.where(core == 0, low, high)[None]

    below, across, diagonal = sent(2, 1, 0), sent(1, 0, 1), sent(3, 1, 1)
    own = [x + y for x, y in zip(quarter(0), halves(below))]
    o_near[1], o_far[1] = after((o_near[1], o_far[1]), own)
    handed = joined(o_near, o_far)
    diagonal = after(diagonal, handed)
    other = [x + y for x, y in zip(halves(across), halves(diagonal))]
    grad_query = joined(dq_near, [pair_swap(x) for x in dq_far])
    grad_key, grad_value = (
        joined([x[:, columns] for x in own], [x[:, columns] for x in other])
        for columns in (slice(0, HEAD_DIM), slice(HEAD_DIM, 2 * HEAD_DIM))
    )
    return handed, grad_query, grad_key, grad_value


def solution(mesh):
    tokens = P("section", "ctx", None)
    return jax.shard_map(
        body,
        mesh=mesh,
        in_specs=(tokens,) * 4 + (P(),),
        out_specs=(tokens,) * 4,
        check_vma=False,
    )
```
